32 devices in a mesh: leaf: 8 (over z, y), panel: 4 (over x, core).
Axes of the slice: x: 2, y: 2, z: 4, core: 2. Of those that a mesh axis runs over, the one named last changes fastest.
Arguments:
- subtree_solution: bfloat16 [32, 4, 16384], P(None, 'panel', 'leaf'), may hold values from -6 to 6
- subtree_coupling: bfloat16 [4, 1024, 2048], P('panel', 'leaf'), may hold values from -0.25 to 0.25
- sub_map: int32 [4, 1024], P('panel', 'leaf'), may hold values from 0 to 8191
- sub_count: int32 [4, 8], P('panel', 'leaf'), may hold values from 1 to 128, 512 in all within a row
- front_rhs: float32 [32, 4, 8192], P(None, 'panel', 'leaf'), may hold values from -6 to 6
- sep_inverse: bfloat16 [4, 8192, 8192], P('panel', None, 'leaf'), may hold values from -0.0625 to 0.0625
- border_coupling: bfloat16 [4, 8192, 2048], P('panel', 'leaf'), may hold values from -0.0625 to 0.0625
- border_map: int32 [4, 2048], replicated, may hold values from 0 to 10239
- root_rhs: float32 [32, 10240], P(None, 'panel'), may hold values from -6 to 6
- root_inverse: bfloat16 [10240, 10240], P('leaf', 'panel'), may hold values from -0.0625 to 0.0625
Outputs:
- root_forward: float32 [32, 10240], P(None, 'leaf')
- root_solution: float32 [32, 10240], P(None, 'panel')
- front_solution: float32 [32, 4, 8192], P(None, 'panel', 'leaf')
- subtree_update: float32 [32, 4, 16384], P(None, 'panel', 'leaf')
The draws below stay inside these ranges and needn't reach their ends.
Inputs may be any that keep to these rules, and one draw needn't show every extreme that they name: `sub_map`: only the first sub_count entries of a subtree's rows are live. `sub_count`: over one front's 8 subtrees the counts sum to 512.
All inputs are finite; a program needn't handle non-finite values. No bound on the sum of `sub_count` on one device may be relied on, other than what follows from the above.
Results may differ from the reference program's by a relative error of at most 0.0075.
Values may be sent and summed in bfloat16 or wider, within the bound.
A program may use at most 64 MiB of HBM per device.

```python
import math
import jax
import jax.numpy as jnp
import numpy as np

RHS_COUNT = 32
S1 = 10240
S2 = 8192
E2 = 2048
SUBTREE_TOP_ROWS = 2048
COUPLING_ROWS = 128
LEVEL_TWO_FRONTS = 4
N_LEAF = 8


def with_ends(array, stream_key, low, high):
    extent = array.shape
    spot = [jax.random.randint(jax.random.fold_in(stream_key, axis), (), 0, extent[axis]) for axis in range(len(extent))]
    array = array.at[tuple(spot)].set(low)
    longest = extent.index(max(extent))
    spot[longest] = (spot[longest] + 1) % extent[longest]
    return array.at[tuple(spot)].set(high)


def levels(stream_key, shape, pieces, least, largest):
    loudness, own = 1.0, jax.random.fold_in(stream_key, 6)
    for axis_at, parts in pieces:
        draws = jnp.exp(jax.random.uniform(jax.random.fold_in(own, axis_at), (parts,), jnp.float32, least / len(pieces), largest / len(pieces)))
        loudness = loudness * jnp.repeat(draws, shape[axis_at] // parts).reshape([-1 if axis == axis_at else 1 for axis in range(len(shape))])
    return loudness


def profile(amount, total, bound, lean):
    weights = [(1 << 20) // math.isqrt(standing ** lean) + 1 for standing in range(2, amount + 1)]
    surplus, given = total - bound - (amount - 1), [1] * (amount - 1)
    while surplus > 0:
        movable = [i for i in range(amount - 1) if given[i] < bound]
        mass, left = sum([weights[i] for i in movable]), surplus
        for i in movable:
            extra = min(bound - given[i], max(1, left * weights[i] // mass), surplus)
            given[i] = given[i] + extra
            surplus = surplus - extra
    return np.array([bound] + given)


def uneven(rng, number_of, total, limit, slope):
    if number_of == 2:
        one = jax.random.randint(rng, (), max(1, total - limit), min(limit, total - 1) + 1)
        return jnp.stack([one, total - one])
    tallies = jnp.asarray(profile(number_of, total, limit, slope), jnp.int32)
    couples = (number_of - 1) // 2
    giver, sink = tallies[1:1 + 2 * couples:2], tallies[2:2 + 2 * couples:2]
    room = jnp.minimum(giver - 1, limit - sink)
    passed = jax.random.randint(jax.random.fold_in(rng, 1), (couples,), 0, 1 << 20) % (room + 1)
    tallies = tallies.at[1:1 + 2 * couples:2].set(giver - passed).at[2:2 + 2 * couples:2].set(sink + passed)
    return tallies[jax.random.permutation(jax.random.fold_in(rng, 2), number_of)]


def normal_values(stream_key, extent, spread, limit, shards=(), kind=jnp.bfloat16):
    result = spread * jax.random.normal(stream_key, extent, jnp.float32)
    if shards:
        result = result * levels(stream_key, extent, shards, -0.22, 0.18)
    return jnp.clip(result, -limit, limit).astype(kind)


def setup_inputs(seed: int = 0) -> dict:
    arg_keys = jax.random.split(jax.random.key(seed), 11)
    return {
        "subtree_solution": normal_values(arg_keys[0], (RHS_COUNT, LEVEL_TWO_FRONTS, N_LEAF * SUBTREE_TOP_ROWS), 1.0, 6.0, ((1, 4), (2, 8))),
        "subtree_coupling": normal_values(arg_keys[1], (LEVEL_TWO_FRONTS, N_LEAF * COUPLING_ROWS, SUBTREE_TOP_ROWS), (SUBTREE_TOP_ROWS // 4) ** -0.5, 0.25, ((0, 4), (1, 8))),
        "sub_map": with_ends(jax.random.randint(arg_keys[2], (LEVEL_TWO_FRONTS, N_LEAF * COUPLING_ROWS), 0, S2), jax.random.fold_in(arg_keys[2], 1), 0, S2 - 1).astype(jnp.int32),
        "sub_count": jax.vmap(lambda own: uneven(own, N_LEAF, N_LEAF * COUPLING_ROWS // 2, COUPLING_ROWS, 2))(jax.random.split(arg_keys[3], LEVEL_TWO_FRONTS)).reshape((LEVEL_TWO_FRONTS, N_LEAF)).astype(jnp.int32),
        "front_rhs": normal_values(arg_keys[4], (RHS_COUNT, LEVEL_TWO_FRONTS, S2), 1.0, 6.0, ((1, 4), (2, 8)), jnp.float32),
        "sep_inverse": normal_values(arg_keys[5], (LEVEL_TWO_FRONTS, S2, S2), S2 ** -0.5, 0.0625, ((0, 4), (2, 8))),
        "border_coupling": normal_values(arg_keys[6], (LEVEL_TWO_FRONTS, S2, E2), S2 ** -0.5, 0.0625, ((0, 4), (1, 8))),
        "border_map": with_ends(jax.random.randint(arg_keys[7], (LEVEL_TWO_FRONTS, E2), 0, S1), jax.random.fold_in(arg_keys[7], 1), 0, S1 - 1).astype(jnp.int32),
        "root_rhs": normal_values(arg_keys[8], (RHS_COUNT, S1), 1.0, 6.0, ((1, 4),), jnp.float32),
        "root_inverse": normal_values(arg_keys[9], (S1, S1), S1 ** -0.5, 0.0625, ((0, 8), (1, 4))),
    }


def reference(subtree_solution, subtree_coupling, sub_map, sub_count, front_rhs, sep_inverse, border_coupling, border_map, root_rhs, root_inverse):
    positions = jnp.arange(COUPLING_ROWS, dtype=jnp.int32)
    forward_list = []
    border_list = []
    coupling_factors = []
    living_list = []
    for front_index in range(LEVEL_TWO_FRONTS):
        solved_values = subtree_solution[:, front_index, :].reshape(RHS_COUNT, N_LEAF, SUBTREE_TOP_ROWS).astype(jnp.float32)
        coupling_factor = subtree_coupling[front_index].reshape(N_LEAF, COUPLING_ROWS, SUBTREE_TOP_ROWS).astype(jnp.float32)
        living = positions[None, :] < sub_count[front_index][:, None]
        contrib = jnp.einsum("rls,ljs->rlj", solved_values, coupling_factor)
        contrib = jnp.where(living[None, :, :], contrib, jnp.zeros_like(contrib))
        extended = jnp.zeros((RHS_COUNT, S2), jnp.float32).at[:, sub_map[front_index]].add(contrib.reshape(RHS_COUNT, N_LEAF * COUPLING_ROWS))
        assembled = (front_rhs[:, front_index, :] - extended).astype(jnp.bfloat16)
        forward = jnp.dot(assembled, sep_inverse[front_index].T, preferred_element_type=jnp.float32)
        border_term = jnp.dot(forward.astype(jnp.bfloat16), border_coupling[front_index], preferred_element_type=jnp.float32)
        forward_list.append(forward)
        border_list.append(border_term)
        coupling_factors.append(coupling_factor)
        living_list.append(living)
    border_all = jnp.stack(border_list, axis=1).reshape(RHS_COUNT, LEVEL_TWO_FRONTS * E2)
    root_term = jnp.zeros((RHS_COUNT, S1), jnp.float32).at[:, border_map.reshape(-1)].add(border_all)
    root_assembled = (root_rhs - root_term).astype(jnp.bfloat16)
    root_forward = jnp.dot(root_assembled, root_inverse.T, preferred_element_type=jnp.float32)
    root_solution = jnp.dot(root_forward.astype(jnp.bfloat16), root_inverse, preferred_element_type=jnp.float32)
    root_half = root_solution.astype(jnp.bfloat16)
    solution_list = []
    update_list = []
    for front_index in range(LEVEL_TWO_FRONTS):
        picked = root_half[:, border_map[front_index]]
        residual = forward_list[front_index] - jnp.dot(picked, border_coupling[front_index].T, preferred_element_type=jnp.float32)
        solution = jnp.dot(residual.astype(jnp.bfloat16), sep_inverse[front_index], preferred_element_type=jnp.float32)
        front_half = solution.astype(jnp.bfloat16)
        gathered_values = front_half[:, sub_map[front_index]].reshape(RHS_COUNT, N_LEAF, COUPLING_ROWS).astype(jnp.float32)
        gathered_values = jnp.where(living_list[front_index][None, :, :], gathered_values, jnp.zeros_like(gathered_values))
        update_term = jnp.einsum("fvq,vqo->fvo", gathered_values, coupling_factors[front_index]).reshape(RHS_COUNT, N_LEAF * SUBTREE_TOP_ROWS)
        solution_list.append(solution)
        update_list.append(update_term)
    front_solution = jnp.stack(solution_list, axis=1)
    subtree_update = jnp.stack(update_list, axis=1)
    return root_forward, root_solution, front_solution, subtree_update
```

```python
import functools
import jax
import jax.numpy as jnp
from jax import lax
from jax.experimental import pallas as pl
from jax.experimental.pallas import tpu as pltpu
from jax.sharding import PartitionSpec as P

MESH = pl.DeviceIdType.MESH
BF = jnp.bfloat16
F32 = jnp.float32
LANES = 128
VMEM_BYTES = 56 * 1024 * 1024
(CON, MAP, FWD, BOR, BPAN, RRS, RAG, RFP, SRS, SAG, PPAN, PAG, RES, PICK) = range(14)
PANEL_PHASES = (BPAN, RFP, PPAN)


def nn(a, b):
    return jnp.dot(a, b, preferred_element_type=F32)


def nt(a, b):
    return lax.dot_general(a, b, (((1,), (1,)), ((), ())), preferred_element_type=F32)


def ceil_to(value, step):
    return -(-value // step) * step


def kernel(
    n_leaf, n_panel,
    ss_ref, sc_ref, map_ref, count_ref, rhs_ref, bmap_ref, root_rhs_ref,
    slab_hbm, border_hbm, root_hbm,
    rf_out, rs_out, fs_out, su_out,
    slab, border, root, oh_sub, oh_root, rhs_pad, forward, picks_send,
    con_l, map_l, fwd_s, fwd_l, bor_s, bor_l, bpan_l, rrs_s, rrs_l, rag_l,
    rfp_l, srs_s, srs_l, sag_l, ppan_s, ppan_l, pag_l, res_l, pick_l,
    load_sem, send_sem, recv_sem,
):
    leaf = lax.axis_index("leaf")
    panel = lax.axis_index("panel")
    batch = ss_ref.shape[0]
    own = rhs_ref.shape[1]
    eblk = bor_l.shape[2]
    blk = rrs_l.shape[2]
    cols = root_rhs_ref.shape[1]
    rows_sub = sc_ref.shape[0]

    loads = [
        pltpu.make_async_copy(slab_hbm, slab, load_sem.at[0]),
        pltpu.make_async_copy(border_hbm, border, load_sem.at[1]),
        pltpu.make_async_copy(root_hbm, root, load_sem.at[2]),
    ]
    for load in loads:
        load.start()

    barrier = pltpu.get_barrier_semaphore()
    for d in range(1, n_leaf):
        pl.semaphore_signal(
            barrier, inc=1, device_id=(lax.rem(leaf + d, n_leaf), panel), device_id_type=MESH
        )
    for d in range(1, n_panel):
        pl.semaphore_signal(
            barrier, inc=1, device_id=(leaf, lax.rem(panel + d, n_panel)), device_id_type=MESH
        )

    def copy(phase, src, dst, peer):
        on_panel = phase in PANEL_PHASES
        me = panel if on_panel else leaf
        target = (leaf, peer) if on_panel else (peer, panel)
        return pltpu.make_async_remote_copy(
            src_ref=src, dst_ref=dst.at[me],
            send_sem=send_sem.at[phase, peer], recv_sem=recv_sem.at[phase, me],
            device_id=target, device_id_type=MESH,
        )

    def group(phase):
        return (panel, n_panel) if phase in PANEL_PHASES else (leaf, n_leaf)

    def send_all(phase, source, dst):
        me, n = group(phase)

        def step(d, carry):
            peer = lax.rem(me + d, n)
            copy(phase, source(peer), dst, peer).start()
            return carry

        lax.fori_loop(1, n, step, 0)

    def arrived(phase, dst, source):
        pltpu.make_async_copy(dst.at[source], dst.at[source], recv_sem.at[phase, source]).wait()

    def arrive_all(phase, dst):
        me, n = group(phase)

        def step(d, carry):
            arrived(phase, dst, lax.rem(me - d + n, n))
            return carry

        lax.fori_loop(1, n, step, 0)

    def sent_all(phase, dst):
        me, n = group(phase)

        def step(d, carry):
            peer = lax.rem(me + d, n)
            pltpu.make_async_copy(dst.at[me], dst.at[me], send_sem.at[phase, peer]).wait()
            return carry

        lax.fori_loop(1, n, step, 0)

    def total(dst):
        result = dst[0].astype(F32)
        for s in range(1, dst.shape[0]):
            result = result + dst[s].astype(F32)
        return result

    def joined(dst):
        return jnp.concatenate([dst[s] for s in range(dst.shape[0])], axis=1)

    def spread_blocks(dst, value):
        for s in range(n_leaf):
            width = max(0, min(blk, cols - s * blk))
            if width:
                dst[s, :, :width] = value[:, s * blk:s * blk + width].astype(dst.dtype)
            if width < blk:
                dst[s, :, width:] = jnp.zeros((batch, blk - width), dst.dtype)

    map_l[leaf] = jnp.broadcast_to(map_ref[...], map_l.shape[1:])
    contrib = nt(ss_ref[...], sc_ref[...])
    living = lax.broadcasted_iota(jnp.int32, (batch, rows_sub), 1) < count_ref[0, 0]
    contrib = jnp.where(living, contrib, 0.0)
    high = contrib.astype(BF)
    con_l[leaf, :batch] = high
    con_l[leaf, batch:] = (contrib - high.astype(F32)).astype(BF)

    pl.semaphore_wait(barrier, n_leaf - 1 + n_panel - 1)
    send_all(MAP, lambda peer: map_l.at[leaf], map_l)
    send_all(CON, lambda peer: con_l.at[leaf], con_l)

    spread_blocks(rhs_pad, root_rhs_ref[...])
    for f in range(n_panel):
        row = bmap_ref[f:f + 1, pl.ds(pl.multiple_of(leaf * eblk, LANES), eblk)]

        def mark_root(c, carry, f=f, row=row):
            at = pl.multiple_of(c * LANES, LANES)
            column = lax.broadcasted_iota(jnp.int32, (LANES, eblk), 0) + (panel * cols + at)
            oh_root[pl.ds(at, LANES), f * eblk:(f + 1) * eblk] = jnp.where(
                column == row, 1.0, 0.0
            ).astype(BF)
            return carry

        lax.fori_loop(0, cols // LANES, mark_root, 0)

    arrive_all(MAP, map_l)

    for s in range(n_leaf):
        def mark_sub(c, carry, s=s):
            at = pl.multiple_of(c * LANES, LANES)
            column = lax.broadcasted_iota(jnp.int32, (LANES, rows_sub), 0) + (leaf * own + at)
            oh_sub[pl.ds(at, LANES), s * rows_sub:(s + 1) * rows_sub] = jnp.where(
                column == map_l[s, 0:1, :], 1.0, 0.0
            ).astype(BF)
            return carry

        lax.fori_loop(0, own // LANES, mark_sub, 0)

    arrive_all(CON, con_l)
    both = nt(joined(con_l), oh_sub[...])
    assembled = (rhs_ref[...] - (both[:batch] + both[batch:])).astype(BF)

    loads[0].wait()

    def forward_step(d, carry):
        peer = lax.rem(leaf + d, n_leaf)
        rows = slab[pl.ds(pl.multiple_of(peer * own, LANES), own), :]
        fwd_s[peer] = nt(assembled, rows).astype(BF)
        copy(FWD, fwd_s.at[peer], fwd_l, peer).start()
        return carry

    lax.fori_loop(1, n_leaf, forward_step, 0)
    mine = nt(assembled, slab[pl.ds(pl.multiple_of(leaf * own, LANES), own), :])
    fwd_l[leaf] = jnp.zeros((batch, own), BF)
    arrive_all(FWD, fwd_l)
    fwd = mine + total(fwd_l)
    forward[...] = fwd
    fwd_half = fwd.astype(BF)

    loads[1].wait()

    def border_step(d, carry):
        peer = lax.rem(leaf + d, n_leaf)
        part = nn(fwd_half, border[:, pl.ds(pl.multiple_of(peer * eblk, LANES), eblk)])
        bor_s[peer] = part.astype(BF)
        copy(BOR, bor_s.at[peer], bor_l, peer).start()
        return carry

    lax.fori_loop(1, n_leaf, border_step, 0)
    own_border = nn(fwd_half, border[:, pl.ds(pl.multiple_of(leaf * eblk, LANES), eblk)])
    bor_l[leaf] = jnp.zeros((batch, eblk), BF)
    arrive_all(BOR, bor_l)
    bpan_l[panel] = (own_border + total(bor_l)).astype(BF)
    send_all(BPAN, lambda peer: bpan_l.at[panel], bpan_l)
    arrive_all(BPAN, bpan_l)

    spread_blocks(rrs_s, nt(joined(bpan_l), oh_root[...]))
    send_all(RRS, lambda peer: rrs_s.at[peer], rrs_l)
    rrs_l[leaf] = rrs_s[leaf]
    arrive_all(RRS, rrs_l)
    rag_l[leaf] = (rhs_pad[leaf] - total(rrs_l)).astype(BF)
    send_all(RAG, lambda peer: rag_l.at[leaf], rag_l)
    loads[2].wait()
    arrive_all(RAG, rag_l)

    rfp_l[panel] = nt(joined(rag_l)[:, :cols], root[...]).astype(BF)
    send_all(RFP, lambda peer: rfp_l.at[panel], rfp_l)
    arrive_all(RFP, rfp_l)
    root_forward = total(rfp_l)
    rf_out[...] = root_forward
    spread_blocks(srs_s, nn(root_forward.astype(BF), root[...]))
    send_all(SRS, lambda peer: srs_s.at[peer], srs_l)
    srs_l[leaf] = srs_s[leaf]
    arrive_all(SRS, srs_l)
    sag_l[leaf] = total(srs_l).astype(BF)
    send_all(SAG, lambda peer: sag_l.at[leaf], sag_l)
    arrive_all(SAG, sag_l)
    root_half = joined(sag_l)[:, :cols]
    rs_out[...] = root_half.astype(F32)

    values = nn(root_half, oh_root[...]).astype(BF)
    for f in range(n_panel):
        ppan_s[f] = values[:, f * eblk:(f + 1) * eblk]
    send_all(PPAN, lambda peer: ppan_s.at[peer], ppan_l)
    ppan_l[panel] = ppan_s[panel]
    arrive_all(PPAN, ppan_l)
    pag_l[leaf] = total(ppan_l).astype(BF)
    send_all(PAG, lambda peer: pag_l.at[leaf], pag_l)
    arrive_all(PAG, pag_l)

    residual = forward[...] - nt(joined(pag_l), border[...])
    res_l[leaf] = residual.astype(BF)
    send_all(RES, lambda peer: res_l.at[leaf], res_l)
    fs_out[...] = nn(res_l[leaf], slab[pl.ds(pl.multiple_of(leaf * own, LANES), own), :])

    def back_step(d, carry):
        source = lax.rem(leaf - d + n_leaf, n_leaf)
        arrived(RES, res_l, source)
        fs_out[...] += nn(res_l[source], slab[pl.ds(pl.multiple_of(source * own, LANES), own), :])
        return carry

    lax.fori_loop(1, n_leaf, back_step, 0)

    picks = nn(fs_out[...].astype(BF), oh_sub[...]).astype(BF)
    for s in range(n_leaf):
        picks_send[s] = picks[:, s * rows_sub:(s + 1) * rows_sub]
    send_all(PICK, lambda peer: picks_send.at[peer], pick_l)
    pick_l[leaf] = picks_send[leaf]
    arrive_all(PICK, pick_l)
    picked = jnp.where(living, total(pick_l), 0.0).astype(BF)
    su_out[...] = nn(picked, sc_ref[...])

    for phase, dst in (
        (MAP, map_l), (CON, con_l), (FWD, fwd_l), (BOR, bor_l), (BPAN, bpan_l), (RRS, rrs_l),
        (RAG, rag_l), (RFP, rfp_l), (SRS, srs_l), (SAG, sag_l), (PPAN, ppan_l), (PAG, pag_l),
        (RES, res_l), (PICK, pick_l),
    ):
        sent_all(phase, dst)


def fused(
    subtree_solution, subtree_coupling, sub_map, sub_count, front_rhs,
    sep_inverse, border_coupling, border_map, root_rhs, root_inverse,
):
    n_leaf, n_panel = lax.axis_size("leaf"), lax.axis_size("panel")
    batch = subtree_solution.shape[0]
    rows_sub, top = subtree_coupling.shape[1:]
    _, sep_width, own = sep_inverse.shape
    e_width = border_coupling.shape[2]
    eblk = e_width // n_leaf
    root_rows, cols = root_inverse.shape
    blk = ceil_to(-(-cols // n_leaf), LANES)
    vmem = pl.BlockSpec(memory_space=pltpu.VMEM)
    anywhere = pl.BlockSpec(memory_space=pl.ANY)
    smem = pl.BlockSpec(memory_space=pltpu.SMEM)

    def slots(n, width, dtype=BF, rows=batch):
        return pltpu.VMEM((n, rows, width), dtype)

    results = pl.pallas_call(
        functools.partial(kernel, n_leaf, n_panel),
        out_shape=(
            jax.ShapeDtypeStruct((batch, root_rows), F32),
            jax.ShapeDtypeStruct((batch, cols), F32),
            jax.ShapeDtypeStruct((batch, own), F32),
            jax.ShapeDtypeStruct((batch, top), F32),
        ),
        in_specs=[vmem, vmem, vmem, smem, vmem, vmem, vmem, anywhere, anywhere, anywhere],
        out_specs=(vmem,) * 4,
        scratch_shapes=[
            pltpu.VMEM((sep_width, own), BF),
            pltpu.VMEM((own, e_width), BF),
            pltpu.VMEM((root_rows, cols), BF),
            pltpu.VMEM((own, n_leaf * rows_sub), BF),
            pltpu.VMEM((cols, n_panel * eblk), BF),
            slots(n_leaf, blk, F32),
            pltpu.VMEM((batch, own), F32),
            slots(n_leaf, rows_sub),
            slots(n_leaf, rows_sub, BF, 2 * batch),
            slots(n_leaf, rows_sub, jnp.int32, 8),
            slots(n_leaf, own), slots(n_leaf, own),
            slots(n_leaf, eblk), slots(n_leaf, eblk),
            slots(n_panel, eblk),
            slots(n_leaf, blk), slots(n_leaf, blk), slots(n_leaf, blk),
            slots(n_panel, root_rows),
            slots(n_leaf, blk), slots(n_leaf, blk), slots(n_leaf, blk),
            slots(n_panel, eblk), slots(n_panel, eblk),
            slots(n_leaf, eblk),
            slots(n_leaf, own),
            slots(n_leaf, rows_sub),
            pltpu.SemaphoreType.DMA((3,)),
            pltpu.SemaphoreType.DMA((14, max(n_leaf, n_panel))),
            pltpu.SemaphoreType.DMA((14, max(n_leaf, n_panel))),
        ],
        compiler_params=pltpu.CompilerParams(
            collective_id=0, has_side_effects=True, vmem_limit_bytes=VMEM_BYTES
        ),
    )(
        subtree_solution[:, 0, :], subtree_coupling[0], sub_map, sub_count, front_rhs[:, 0, :],
        border_map, root_rhs, sep_inverse[0], border_coupling[0], root_inverse,
    )
    root_forward, root_solution, front_solution, update = results
    return root_forward, root_solution, front_solution[:, None, :], update[:, None, :]


def fits(
    subtree_solution, subtree_coupling, sub_map, sub_count, front_rhs,
    sep_inverse, border_coupling, border_map, root_rhs, root_inverse,
):
    n_leaf = lax.axis_size("leaf")
    widths = (
        subtree_coupling.shape[1], subtree_coupling.shape[2], sep_inverse.shape[2],
        border_coupling.shape[2] // n_leaf, root_inverse.shape[0], root_inverse.shape[1],
    )
    small = (sep_inverse.size + border_coupling.size + root_inverse.size) * 2 < VMEM_BYTES * 6 // 10
    return (
        all(width % LANES == 0 for width in widths)
        and subtree_solution.shape[0] % 16 == 0
        and small
    )


def program(*args):
    return fused(*args) if fits(*args) else body(*args)


def body(
    subtree_solution,
    subtree_coupling,
    sub_map,
    sub_count,
    front_rhs,
    sep_inverse,
    border_coupling,
    border_map,
    root_rhs,
    root_inverse,
):
    solved_values = subtree_solution[:, 0, :]
    coupling_factor = subtree_coupling[0]
    rows_sub = coupling_factor.shape[0]
    living = jnp.arange(rows_sub, dtype=jnp.int32) < sub_count[0, 0]
    contrib = lax.dot_general(
        solved_values, coupling_factor, (((1,), (1,)), ((), ())), preferred_element_type=jnp.float32
    )
    contrib = jnp.where(living[None, :], contrib, jnp.zeros_like(contrib))
    slab = sep_inverse[0]
    sep_width = slab.shape[0]
    batch = solved_values.shape[0]
    extended = jnp.zeros((batch, sep_width), jnp.float32).at[:, sub_map[0]].add(contrib)
    arrived = lax.psum_scatter(extended, "leaf", scatter_dimension=1, tiled=True)
    assembled = (front_rhs[:, 0, :] - arrived).astype(jnp.bfloat16)
    partial_rows = lax.dot_general(
        assembled, slab, (((1,), (1,)), ((), ())), preferred_element_type=jnp.float32
    )
    forward = lax.psum_scatter(partial_rows, "leaf", scatter_dimension=1, tiled=True)
    border_rows_local = border_coupling[0]
    partial_border = jnp.dot(
        forward.astype(jnp.bfloat16), border_rows_local, preferred_element_type=jnp.float32
    )
    border_term = lax.psum(partial_border, "leaf")
    panel_index = lax.axis_index("panel")
    col_width = root_rhs.shape[1]
    root_width = col_width * lax.axis_size("panel")
    own_map = border_map[panel_index]
    spread = jnp.zeros((batch, root_width), jnp.float32).at[:, own_map].add(border_term)
    root_term = lax.psum_scatter(spread, "panel", scatter_dimension=1, tiled=True)
    root_assembled = (root_rhs - root_term).astype(jnp.bfloat16)
    root_partial = lax.dot_general(
        root_assembled, root_inverse, (((1,), (1,)), ((), ())), preferred_element_type=jnp.float32
    )
    root_forward = lax.psum(root_partial, "panel")
    column_partial = jnp.dot(
        root_forward.astype(jnp.bfloat16), root_inverse, preferred_element_type=jnp.float32
    )
    root_solution = lax.psum(column_partial, "leaf")
    root_half = root_solution.astype(jnp.bfloat16)
    whole_root = lax.all_gather(root_half, "panel", axis=1, tiled=True)
    border_values = whole_root[:, own_map]
    correction = lax.dot_general(
        border_values,
        border_rows_local,
        (((1,), (1,)), ((), ())),
        preferred_element_type=jnp.float32,
    )
    residual = (forward - correction).astype(jnp.bfloat16)
    front_solution = jnp.dot(
        lax.all_gather(residual, "leaf", axis=1, tiled=True),
        slab,
        preferred_element_type=jnp.float32,
    )
    front_half = front_solution.astype(jnp.bfloat16)
    whole_front = lax.all_gather(front_half, "leaf", axis=1, tiled=True)
    picked = whole_front[:, sub_map[0]]
    picked = jnp.where(living[None, :], picked, jnp.zeros_like(picked))
    subtree_update = jnp.dot(picked, coupling_factor, preferred_element_type=jnp.float32)
    return (root_forward, root_solution, front_solution[:, None, :], subtree_update[:, None, :])


def solution(mesh):
    return jax.shard_map(
        program,
        mesh=mesh,
        in_specs=(
            P(None, "panel", "leaf"),
            P("panel", "leaf", None),
            P("panel", "leaf"),
            P("panel", "leaf"),
            P(None, "panel", "leaf"),
            P("panel", None, "leaf"),
            P("panel", "leaf", None),
            P(),
            P(None, "panel"),
            P("leaf", "panel"),
        ),
        out_specs=(
            P(None, "leaf"),
            P(None, "panel"),
            P(None, "panel", "leaf"),
            P(None, "panel", "leaf"),
        ),
        check_vma=False,
    )
```

```python
import functools
import jax
import jax.numpy as jnp
from jax import lax
from jax.experimental import pallas as pl
from jax.experimental.pallas import tpu as pltpu
from jax.sharding import PartitionSpec as P

MESH = pl.DeviceIdType.MESH
BF = jnp.bfloat16
F32 = jnp.float32
LANES = 128
VMEM_BYTES = 56 * 1024 * 1024
(CON, MAP, FWD, BOR, BPAN, RRS, RAG, RFP, SRS, SAG, PPAN, PAG, RES, PICK) = range(14)
PANEL_PHASES = (BPAN, RFP, PPAN)


def nn(a, b):
    return jnp.dot(a, b, preferred_element_type=F32)


def nt(a, b):
    return lax.dot_general(a, b, (((1,), (1,)), ((), ())), preferred_element_type=F32)


def ceil_to(value, step):
    return -(-value // step) * step


def kernel(
    n_leaf, n_panel,
    ss_ref, sc_ref, map_ref, count_ref, rhs_ref, bmap_ref, root_rhs_ref,
    slab_hbm, border_hbm, root_hbm,
    rf_out, rs_out, fs_out, su_out,
    slab, border, root, oh_sub, oh_root, rhs_pad, forward, picks_send,
    con_l, map_l, fwd_s, fwd_l, bor_s, bor_l, bpan_l, rrs_s, rrs_l, rag_l,
    rfp_l, srs_s, srs_l, sag_l, ppan_s, ppan_l, pag_l, res_l, pick_l,
    slab_sem, load_sem, send_sem, recv_sem,
):
    leaf = lax.axis_index("leaf")
    panel = lax.axis_index("panel")
    batch = ss_ref.shape[0]
    own = rhs_ref.shape[2]
    eblk = bor_l.shape[2]
    blk = rrs_l.shape[2]
    cols = root_rhs_ref.shape[1]
    rows_sub = sc_ref.shape[0]

    def slab_load(block):
        rows = pl.ds(pl.multiple_of(block * own, LANES), own)
        return pltpu.make_async_copy(slab_hbm.at[rows], slab.at[rows], slab_sem.at[block])

    loads = [
        pltpu.make_async_copy(border_hbm, border, load_sem.at[0]),
        pltpu.make_async_copy(root_hbm, root, load_sem.at[1]),
    ]
    for d in range(1, n_leaf + 1):
        slab_load(lax.rem(leaf + d, n_leaf)).start()

    barrier = pltpu.get_barrier_semaphore()
    for d in range(1, n_leaf):
        pl.semaphore_signal(
            barrier, inc=1, device_id=(lax.rem(leaf + d, n_leaf), panel), device_id_type=MESH
        )
    for d in range(1, n_panel):
        pl.semaphore_signal(
            barrier, inc=1, device_id=(leaf, lax.rem(panel + d, n_panel)), device_id_type=MESH
        )

    def copy(phase, src, dst, peer):
        on_panel = phase in PANEL_PHASES
        me = panel if on_panel else leaf
        target = (leaf, peer) if on_panel else (peer, panel)
        return pltpu.make_async_remote_copy(
            src_ref=src, dst_ref=dst.at[me],
            send_sem=send_sem.at[phase, peer], recv_sem=recv_sem.at[phase, me],
            device_id=target, device_id_type=MESH,
        )

    def group(phase):
        return (panel, n_panel) if phase in PANEL_PHASES else (leaf, n_leaf)

    def send_all(phase, source, dst):
        me, n = group(phase)

        def step(d, carry):
            peer = lax.rem(me + d, n)
            copy(phase, source(peer), dst, peer).start()
            return carry

        lax.fori_loop(1, n, step, 0)

    def arrived(phase, dst, source):
        pltpu.make_async_copy(dst.at[source], dst.at[source], recv_sem.at[phase, source]).wait()

    def arrive_all(phase, dst):
        me, n = group(phase)

        def step(d, carry):
            arrived(phase, dst, lax.rem(me - d + n, n))
            return carry

        lax.fori_loop(1, n, step, 0)

    def sent_all(phase, dst):
        me, n = group(phase)

        def step(d, carry):
            peer = lax.rem(me + d, n)
            pltpu.make_async_copy(dst.at[me], dst.at[me], send_sem.at[phase, peer]).wait()
            return carry

        lax.fori_loop(1, n, step, 0)

    def total(dst):
        result = dst[0].astype(F32)
        for s in range(1, dst.shape[0]):
            result = result + dst[s].astype(F32)
        return result

    def joined(dst):
        return jnp.concatenate([dst[s] for s in range(dst.shape[0])], axis=1)

    def spread_blocks(dst, value):
        for s in range(n_leaf):
            width = max(0, min(blk, cols - s * blk))
            if width:
                dst[s, :, :width] = value[:, s * blk:s * blk + width].astype(dst.dtype)
            if width < blk:
                dst[s, :, width:] = jnp.zeros((batch, blk - width), dst.dtype)

    map_l[leaf] = jnp.broadcast_to(map_ref[...], map_l.shape[1:])
    contrib = nt(ss_ref[...], sc_ref[...])
    living = lax.broadcasted_iota(jnp.int32, (batch, rows_sub), 1) < count_ref[0, 0]
    contrib = jnp.where(living, contrib, 0.0)
    high = contrib.astype(BF)
    con_l[leaf, :batch] = high
    con_l[leaf, batch:] = (contrib - high.astype(F32)).astype(BF)

    forward[...] = rhs_ref[:, 0, :]
    pl.semaphore_wait(barrier, n_leaf - 1 + n_panel - 1)
    send_all(MAP, lambda peer: map_l.at[leaf], map_l)
    send_all(CON, lambda peer: con_l.at[leaf], con_l)

    spread_blocks(rhs_pad, root_rhs_ref[...])
    for f in range(n_panel):
        row = bmap_ref[f:f + 1, pl.ds(pl.multiple_of(leaf * eblk, LANES), eblk)]

        def mark_root(c, carry, f=f, row=row):
            at = pl.multiple_of(c * LANES, LANES)
            column = lax.broadcasted_iota(jnp.int32, (LANES, eblk), 0) + (panel * cols + at)
            oh_root[pl.ds(at, LANES), f * eblk:(f + 1) * eblk] = jnp.where(
                column == row, 1.0, 0.0
            ).astype(BF)
            return carry

        lax.fori_loop(0, cols // LANES, mark_root, 0)

    arrive_all(MAP, map_l)

    for s in range(n_leaf):
        def mark_sub(c, carry, s=s):
            at = pl.multiple_of(c * LANES, LANES)
            column = lax.broadcasted_iota(jnp.int32, (LANES, rows_sub), 0) + (leaf * own + at)
            oh_sub[pl.ds(at, LANES), s * rows_sub:(s + 1) * rows_sub] = jnp.where(
                column == map_l[s, 0:1, :], 1.0, 0.0
            ).astype(BF)
            return carry

        lax.fori_loop(0, own // LANES, mark_sub, 0)

    arrive_all(CON, con_l)
    both = nt(joined(con_l), oh_sub[...])
    assembled = (forward[...] - (both[:batch] + both[batch:])).astype(BF)

    def forward_step(d, carry):
        peer = lax.rem(leaf + d, n_leaf)
        slab_load(peer).wait()
        rows = slab[pl.ds(pl.multiple_of(peer * own, LANES), own), :]
        fwd_s[peer] = nt(assembled, rows).astype(BF)
        copy(FWD, fwd_s.at[peer], fwd_l, peer).start()
        return carry

    lax.fori_loop(1, n_leaf, forward_step, 0)
    slab_load(leaf).wait()
    for load in loads:
        load.start()
    mine = nt(assembled, slab[pl.ds(pl.multiple_of(leaf * own, LANES), own), :])
    fwd_l[leaf] = jnp.zeros((batch, own), BF)
    sent_all(MAP, map_l)
    sent_all(CON, con_l)
    arrive_all(FWD, fwd_l)
    fwd = mine + total(fwd_l)
    forward[...] = fwd
    fwd_half = fwd.astype(BF)

    loads[0].wait()

    def border_step(d, carry):
        peer = lax.rem(leaf + d, n_leaf)
        part = nn(fwd_half, border[:, pl.ds(pl.multiple_of(peer * eblk, LANES), eblk)])
        bor_s[peer] = part.astype(BF)
        copy(BOR, bor_s.at[peer], bor_l, peer).start()
        return carry

    lax.fori_loop(1, n_leaf, border_step, 0)
    own_border = nn(fwd_half, border[:, pl.ds(pl.multiple_of(leaf * eblk, LANES), eblk)])
    bor_l[leaf] = jnp.zeros((batch, eblk), BF)
    sent_all(FWD, fwd_l)
    arrive_all(BOR, bor_l)
    bpan_l[panel] = (own_border + total(bor_l)).astype(BF)
    send_all(BPAN, lambda peer: bpan_l.at[panel], bpan_l)
    sent_all(BOR, bor_l)
    arrive_all(BPAN, bpan_l)

    spread_blocks(rrs_s, nt(joined(bpan_l), oh_root[...]))
    send_all(RRS, lambda peer: rrs_s.at[peer], rrs_l)
    rrs_l[leaf] = rrs_s[leaf]
    sent_all(BPAN, bpan_l)
    arrive_all(RRS, rrs_l)
    rag_l[leaf] = (rhs_pad[leaf] - total(rrs_l)).astype(BF)
    send_all(RAG, lambda peer: rag_l.at[leaf], rag_l)
    loads[1].wait()
    sent_all(RRS, rrs_l)
    arrive_all(RAG, rag_l)

    rfp_l[panel] = nt(joined(rag_l)[:, :cols], root[...]).astype(BF)
    send_all(RFP, lambda peer: rfp_l.at[panel], rfp_l)
    sent_all(RAG, rag_l)
    arrive_all(RFP, rfp_l)
    root_forward = total(rfp_l)
    rf_out[...] = root_forward
    spread_blocks(srs_s, nn(root_forward.astype(BF), root[...]))
    send_all(SRS, lambda peer: srs_s.at[peer], srs_l)
    srs_l[leaf] = srs_s[leaf]
    sent_all(RFP, rfp_l)
    arrive_all(SRS, srs_l)
    sag_l[leaf] = total(srs_l).astype(BF)
    send_all(SAG, lambda peer: sag_l.at[leaf], sag_l)
    sent_all(SRS, srs_l)
    arrive_all(SAG, sag_l)
    root_half = joined(sag_l)[:, :cols]
    rs_out[...] = root_half.astype(F32)

    values = nn(root_half, oh_root[...]).astype(BF)
    for f in range(n_panel):
        ppan_s[f] = values[:, f * eblk:(f + 1) * eblk]
    send_all(PPAN, lambda peer: ppan_s.at[peer], ppan_l)
    ppan_l[panel] = ppan_s[panel]
    sent_all(SAG, sag_l)
    arrive_all(PPAN, ppan_l)
    pag_l[leaf] = total(ppan_l).astype(BF)
    send_all(PAG, lambda peer: pag_l.at[leaf], pag_l)
    sent_all(PPAN, ppan_l)
    arrive_all(PAG, pag_l)

    residual = forward[...] - nt(joined(pag_l), border[...])
    res_l[leaf] = residual.astype(BF)
    send_all(RES, lambda peer: res_l.at[leaf], res_l)
    sent_all(PAG, pag_l)
    fs_out[...] = nn(res_l[leaf], slab[pl.ds(pl.multiple_of(leaf * own, LANES), own), :])

    def back_step(d, carry):
        source = lax.rem(leaf - d + n_leaf, n_leaf)
        arrived(RES, res_l, source)
        fs_out[...] += nn(res_l[source], slab[pl.ds(pl.multiple_of(source * own, LANES), own), :])
        return carry

    lax.fori_loop(1, n_leaf, back_step, 0)

    picks = nn(fs_out[...].astype(BF), oh_sub[...]).astype(BF)
    for s in range(n_leaf):
        picks_send[s] = picks[:, s * rows_sub:(s + 1) * rows_sub]
    send_all(PICK, lambda peer: picks_send.at[peer], pick_l)
    pick_l[leaf] = picks_send[leaf]
    sent_all(RES, res_l)
    arrive_all(PICK, pick_l)
    picked = jnp.where(living, total(pick_l), 0.0).astype(BF)
    su_out[...] = nn(picked, sc_ref[...])
    sent_all(PICK, pick_l)


def hand_out(rf_ref, rs_ref, fs_ref, su_ref, rf_out, rs_out, fs_out, su_out):
    rf_out[...] = rf_ref[...]
    rs_out[...] = rs_ref[...]
    fs_out[:, 0, :] = fs_ref[...]
    su_out[:, 0, :] = su_ref[...]


def fused(
    subtree_solution, subtree_coupling, sub_map, sub_count, front_rhs,
    sep_inverse, border_coupling, border_map, root_rhs, root_inverse,
):
    n_leaf, n_panel = lax.axis_size("leaf"), lax.axis_size("panel")
    batch = subtree_solution.shape[0]
    rows_sub, top = subtree_coupling.shape[1:]
    _, sep_width, own = sep_inverse.shape
    e_width = border_coupling.shape[2]
    eblk = e_width // n_leaf
    root_rows, cols = root_inverse.shape
    blk = ceil_to(-(-cols // n_leaf), LANES)
    vmem = pl.BlockSpec(memory_space=pltpu.VMEM)
    anywhere = pl.BlockSpec(memory_space=pl.ANY)
    smem = pl.BlockSpec(memory_space=pltpu.SMEM)

    def slots(n, width, dtype=BF, rows=batch):
        return pltpu.VMEM((n, rows, width), dtype)

    results = pl.pallas_call(
        functools.partial(kernel, n_leaf, n_panel),
        out_shape=(
            jax.ShapeDtypeStruct((batch, root_rows), F32),
            jax.ShapeDtypeStruct((batch, cols), F32),
            jax.ShapeDtypeStruct((batch, own), F32),
            jax.ShapeDtypeStruct((batch, top), F32),
        ),
        in_specs=[vmem, vmem, vmem, smem, vmem, vmem, vmem, anywhere, anywhere, anywhere],
        out_specs=(vmem,) * 4,
        scratch_shapes=[
            pltpu.VMEM((sep_width, own), BF),
            pltpu.VMEM((own, e_width), BF),
            pltpu.VMEM((root_rows, cols), BF),
            pltpu.VMEM((own, n_leaf * rows_sub), BF),
            pltpu.VMEM((cols, n_panel * eblk), BF),
            slots(n_leaf, blk, F32),
            pltpu.VMEM((batch, own), F32),
            slots(n_leaf, rows_sub),
            slots(n_leaf, rows_sub, BF, 2 * batch),
            slots(n_leaf, rows_sub, jnp.int32, 8),
            slots(n_leaf, own), slots(n_leaf, own),
            slots(n_leaf, eblk), slots(n_leaf, eblk),
            slots(n_panel, eblk),
            slots(n_leaf, blk), slots(n_leaf, blk), slots(n_leaf, blk),
            slots(n_panel, root_rows),
            slots(n_leaf, blk), slots(n_leaf, blk), slots(n_leaf, blk),
            slots(n_panel, eblk), slots(n_panel, eblk),
            slots(n_leaf, eblk),
            slots(n_leaf, own),
            slots(n_leaf, rows_sub),
            pltpu.SemaphoreType.DMA((n_leaf,)),
            pltpu.SemaphoreType.DMA((2,)),
            pltpu.SemaphoreType.DMA((14, max(n_leaf, n_panel))),
            pltpu.SemaphoreType.DMA((14, max(n_leaf, n_panel))),
        ],
        compiler_params=pltpu.CompilerParams(
            collective_id=0, has_side_effects=True, vmem_limit_bytes=VMEM_BYTES
        ),
    )(
        subtree_solution[:, 0, :], subtree_coupling[0], sub_map, sub_count, front_rhs,
        border_map, root_rhs, sep_inverse[0], border_coupling[0], root_inverse,
    )
    return pl.pallas_call(
        hand_out,
        out_shape=(
            jax.ShapeDtypeStruct((batch, root_rows), F32),
            jax.ShapeDtypeStruct((batch, cols), F32),
            jax.ShapeDtypeStruct((batch, 1, own), F32),
            jax.ShapeDtypeStruct((batch, 1, top), F32),
        ),
        in_specs=[vmem] * 4,
        out_specs=(vmem,) * 4,
    )(*results)


def fits(
    subtree_solution, subtree_coupling, sub_map, sub_count, front_rhs,
    sep_inverse, border_coupling, border_map, root_rhs, root_inverse,
):
    n_leaf = lax.axis_size("leaf")
    widths = (
        subtree_coupling.shape[1], subtree_coupling.shape[2], sep_inverse.shape[2],
        border_coupling.shape[2] // n_leaf, root_inverse.shape[0], root_inverse.shape[1],
    )
    small = (sep_inverse.size + border_coupling.size + root_inverse.size) * 2 < VMEM_BYTES * 6 // 10
    return (
        all(width % LANES == 0 for width in widths)
        and subtree_solution.shape[0] % 16 == 0
        and small
    )


def program(*args):
    return fused(*args) if fits(*args) else body(*args)


def body(
    subtree_solution,
    subtree_coupling,
    sub_map,
    sub_count,
    front_rhs,
    sep_inverse,
    border_coupling,
    border_map,
    root_rhs,
    root_inverse,
):
    solved_values = subtree_solution[:, 0, :]
    coupling_factor = subtree_coupling[0]
    rows_sub = coupling_factor.shape[0]
    living = jnp.arange(rows_sub, dtype=jnp.int32) < sub_count[0, 0]
    contrib = lax.dot_general(
        solved_values, coupling_factor, (((1,), (1,)), ((), ())), preferred_element_type=jnp.float32
    )
    contrib = jnp.where(living[None, :], contrib, jnp.zeros_like(contrib))
    slab = sep_inverse[0]
    sep_width = slab.shape[0]
    batch = solved_values.shape[0]
    extended = jnp.zeros((batch, sep_width), jnp.float32).at[:, sub_map[0]].add(contrib)
    arrived = lax.psum_scatter(extended, "leaf", scatter_dimension=1, tiled=True)
    assembled = (front_rhs[:, 0, :] - arrived).astype(jnp.bfloat16)
    partial_rows = lax.dot_general(
        assembled, slab, (((1,), (1,)), ((), ())), preferred_element_type=jnp.float32
    )
    forward = lax.psum_scatter(partial_rows, "leaf", scatter_dimension=1, tiled=True)
    border_rows_local = border_coupling[0]
    partial_border = jnp.dot(
        forward.astype(jnp.bfloat16), border_rows_local, preferred_element_type=jnp.float32
    )
    border_term = lax.psum(partial_border, "leaf")
    panel_index = lax.axis_index("panel")
    col_width = root_rhs.shape[1]
    root_width = col_width * lax.axis_size("panel")
    own_map = border_map[panel_index]
    spread = jnp.zeros((batch, root_width), jnp.float32).at[:, own_map].add(border_term)
    root_term = lax.psum_scatter(spread, "panel", scatter_dimension=1, tiled=True)
    root_assembled = (root_rhs - root_term).astype(jnp.bfloat16)
    root_partial = lax.dot_general(
        root_assembled, root_inverse, (((1,), (1,)), ((), ())), preferred_element_type=jnp.float32
    )
    root_forward = lax.psum(root_partial, "panel")
    column_partial = jnp.dot(
        root_forward.astype(jnp.bfloat16), root_inverse, preferred_element_type=jnp.float32
    )
    root_solution = lax.psum(column_partial, "leaf")
    root_half = root_solution.astype(jnp.bfloat16)
    whole_root = lax.all_gather(root_half, "panel", axis=1, tiled=True)
    border_values = whole_root[:, own_map]
    correction = lax.dot_general(
        border_values,
        border_rows_local,
        (((1,), (1,)), ((), ())),
        preferred_element_type=jnp.float32,
    )
    residual = (forward - correction).astype(jnp.bfloat16)
    front_solution = jnp.dot(
        lax.all_gather(residual, "leaf", axis=1, tiled=True),
        slab,
        preferred_element_type=jnp.float32,
    )
    front_half = front_solution.astype(jnp.bfloat16)
    whole_front = lax.all_gather(front_half, "leaf", axis=1, tiled=True)
    picked = whole_front[:, sub_map[0]]
    picked = jnp.where(living[None, :], picked, jnp.zeros_like(picked))
    subtree_update = jnp.dot(picked, coupling_factor, preferred_element_type=jnp.float32)
    return (root_forward, root_solution, front_solution[:, None, :], subtree_update[:, None, :])


def solution(mesh):
    return jax.shard_map(
        program,
        mesh=mesh,
        in_specs=(
            P(None, "panel", "leaf"),
            P("panel", "leaf", None),
            P("panel", "leaf"),
            P("panel", "leaf"),
            P(None, "panel", "leaf"),
            P("panel", None, "leaf"),
            P("panel", "leaf", None),
            P(),
            P(None, "panel"),
            P("leaf", "panel"),
        ),
        out_specs=(
            P(None, "leaf"),
            P(None, "panel"),
            P(None, "panel", "leaf"),
            P(None, "panel", "leaf"),
        ),
        check_vma=False,
    )
```

```python
import functools
import jax
import jax.numpy as jnp
from jax import lax
from jax.experimental import pallas as pl
from jax.experimental.pallas import tpu as pltpu
from jax.sharding import PartitionSpec as P

MESH = pl.DeviceIdType.MESH
BF = jnp.bfloat16
F32 = jnp.float32
LANES = 128
VMEM_BYTES = 56 * 1024 * 1024
(CON, MAP, FWD, BOR, BPAN, RRS, RAG, RFP, SRS, SAG, PPAN, PAG, RES, PICK) = range(14)
PANEL_PHASES = (BPAN, RFP, PPAN)


def nn(a, b):
    return jnp.dot(a, b, preferred_element_type=F32)


def nt(a, b):
    return lax.dot_general(a, b, (((1,), (1,)), ((), ())), preferred_element_type=F32)


def ceil_to(value, step):
    return -(-value // step) * step


def kernel(
    n_leaf, n_panel,
    ss_ref, sc_ref, map_ref, count_ref, rhs_ref, bmap_ref, root_rhs_ref,
    slab_hbm, border_hbm, root_hbm,
    rf_out, rs_out, fs_out, su_out,
    slab, border, root, oh_sub, oh_root, rhs_pad, forward, picks_send,
    con_l, map_l, fwd_s, fwd_l, bor_s, bor_l, bpan_l, rrs_s, rrs_l, rag_l,
    rfp_l, srs_s, srs_l, sag_l, ppan_s, ppan_l, pag_l, res_l, pick_l,
    slab_sem, load_sem, send_sem, recv_sem,
):
    leaf = lax.axis_index("leaf")
    panel = lax.axis_index("panel")
    batch = ss_ref.shape[0]
    own = rhs_ref.shape[2]
    eblk = bor_l.shape[2]
    blk = rrs_l.shape[2]
    cols = root_rhs_ref.shape[1]
    rows_sub = sc_ref.shape[0]

    def slab_load(block):
        rows = pl.ds(pl.multiple_of(block * own, LANES), own)
        return pltpu.make_async_copy(slab_hbm.at[rows], slab.at[rows], slab_sem.at[block])

    loads = [
        pltpu.make_async_copy(border_hbm, border, load_sem.at[0]),
        pltpu.make_async_copy(root_hbm, root, load_sem.at[1]),
    ]
    for d in range(1, n_leaf + 1):
        slab_load(lax.rem(leaf + d, n_leaf)).start()

    barrier = pltpu.get_barrier_semaphore()
    for d in range(1, n_leaf):
        pl.semaphore_signal(
            barrier, inc=1, device_id=(lax.rem(leaf + d, n_leaf), panel), device_id_type=MESH
        )
    for d in range(1, n_panel):
        pl.semaphore_signal(
            barrier, inc=1, device_id=(leaf, lax.rem(panel + d, n_panel)), device_id_type=MESH
        )

    def copy(phase, src, dst, peer):
        on_panel = phase in PANEL_PHASES
        me = panel if on_panel else leaf
        target = (leaf, peer) if on_panel else (peer, panel)
        return pltpu.make_async_remote_copy(
            src_ref=src, dst_ref=dst.at[me],
            send_sem=send_sem.at[phase, peer], recv_sem=recv_sem.at[phase, me],
            device_id=target, device_id_type=MESH,
        )

    def group(phase):
        return (panel, n_panel) if phase in PANEL_PHASES else (leaf, n_leaf)

    def send_all(phase, source, dst):
        me, n = group(phase)

        def step(d, carry):
            peer = lax.rem(me + d, n)
            copy(phase, source(peer), dst, peer).start()
            return carry

        lax.fori_loop(1, n, step, 0)

    def arrived(phase, dst, source):
        pltpu.make_async_copy(dst.at[source], dst.at[source], recv_sem.at[phase, source]).wait()

    def arrive_all(phase, dst):
        me, n = group(phase)

        def step(d, carry):
            arrived(phase, dst, lax.rem(me - d + n, n))
            return carry

        lax.fori_loop(1, n, step, 0)

    def sent_all(phase, dst):
        me, n = group(phase)

        def step(d, carry):
            peer = lax.rem(me + d, n)
            pltpu.make_async_copy(dst.at[me], dst.at[me], send_sem.at[phase, peer]).wait()
            return carry

        lax.fori_loop(1, n, step, 0)

    def total(dst):
        result = dst[0].astype(F32)
        for s in range(1, dst.shape[0]):
            result = result + dst[s].astype(F32)
        return result

    def joined(dst):
        return jnp.concatenate([dst[s] for s in range(dst.shape[0])], axis=1)

    def spread_blocks(dst, value):
        for s in range(n_leaf):
            width = max(0, min(blk, cols - s * blk))
            if width:
                dst[s, :, :width] = value[:, s * blk:s * blk + width].astype(dst.dtype)
            if width < blk:
                dst[s, :, width:] = jnp.zeros((batch, blk - width), dst.dtype)

    map_l[leaf] = jnp.broadcast_to(map_ref[...], map_l.shape[1:])
    contrib = nt(ss_ref[...], sc_ref[...])
    living = lax.broadcasted_iota(jnp.int32, (batch, rows_sub), 1) < count_ref[0, 0]
    contrib = jnp.where(living, contrib, 0.0)
    high = contrib.astype(BF)
    con_l[leaf, :batch] = high
    con_l[leaf, batch:] = (contrib - high.astype(F32)).astype(BF)

    forward[...] = rhs_ref[:, 0, :]
    pl.semaphore_wait(barrier, n_leaf - 1 + n_panel - 1)
    send_all(MAP, lambda peer: map_l.at[leaf], map_l)
    send_all(CON, lambda peer: con_l.at[leaf], con_l)

    spread_blocks(rhs_pad, root_rhs_ref[...])
    for f in range(n_panel):
        row = bmap_ref[f:f + 1, pl.ds(pl.multiple_of(leaf * eblk, LANES), eblk)]

        def mark_root(c, carry, f=f, row=row):
            at = pl.multiple_of(c * LANES, LANES)
            column = lax.broadcasted_iota(jnp.int32, (LANES, eblk), 0) + (panel * cols + at)
            oh_root[pl.ds(at, LANES), f * eblk:(f + 1) * eblk] = jnp.where(
                column == row, 1.0, 0.0
            ).astype(BF)
            return carry

        lax.fori_loop(0, cols // LANES, mark_root, 0)

    arrive_all(MAP, map_l)

    for s in range(n_leaf):
        def mark_sub(c, carry, s=s):
            at = pl.multiple_of(c * LANES, LANES)
            column = lax.broadcasted_iota(jnp.int32, (LANES, rows_sub), 0) + (leaf * own + at)
            oh_sub[pl.ds(at, LANES), s * rows_sub:(s + 1) * rows_sub] = jnp.where(
                column == map_l[s, 0:1, :], 1.0, 0.0
            ).astype(BF)
            return carry

        lax.fori_loop(0, own // LANES, mark_sub, 0)

    arrive_all(CON, con_l)
    both = nt(joined(con_l), oh_sub[...])
    assembled = (forward[...] - (both[:batch] + both[batch:])).astype(BF)

    def forward_step(d, carry):
        peer = lax.rem(leaf + d, n_leaf)
        slab_load(peer).wait()
        rows = slab[pl.ds(pl.multiple_of(peer * own, LANES), own), :]
        fwd_s[peer] = nt(assembled, rows).astype(BF)
        copy(FWD, fwd_s.at[peer], fwd_l, peer).start()
        return carry

    lax.fori_loop(1, n_leaf, forward_step, 0)
    slab_load(leaf).wait()
    for load in loads:
        load.start()
    mine = nt(assembled, slab[pl.ds(pl.multiple_of(leaf * own, LANES), own), :])
    fwd_l[leaf] = jnp.zeros((batch, own), BF)
    sent_all(MAP, map_l)
    sent_all(CON, con_l)
    arrive_all(FWD, fwd_l)
    fwd = mine + total(fwd_l)
    forward[...] = fwd
    fwd_half = fwd.astype(BF)

    loads[0].wait()

    def border_step(d, carry):
        peer = lax.rem(leaf + d, n_leaf)
        part = nn(fwd_half, border[:, pl.ds(pl.multiple_of(peer * eblk, LANES), eblk)])
        bor_s[peer] = part.astype(BF)
        copy(BOR, bor_s.at[peer], bor_l, peer).start()
        return carry

    lax.fori_loop(1, n_leaf, border_step, 0)
    own_border = nn(fwd_half, border[:, pl.ds(pl.multiple_of(leaf * eblk, LANES), eblk)])
    bor_l[leaf] = jnp.zeros((batch, eblk), BF)
    sent_all(FWD, fwd_l)
    arrive_all(BOR, bor_l)
    bpan_l[panel] = (own_border + total(bor_l)).astype(BF)
    send_all(BPAN, lambda peer: bpan_l.at[panel], bpan_l)
    sent_all(BOR, bor_l)
    arrive_all(BPAN, bpan_l)

    spread_blocks(rrs_s, nt(joined(bpan_l), oh_root[...]))
    send_all(RRS, lambda peer: rrs_s.at[peer], rrs_l)
    rrs_l[leaf] = rrs_s[leaf]
    sent_all(BPAN, bpan_l)
    arrive_all(RRS, rrs_l)
    rag_l[leaf] = (rhs_pad[leaf] - total(rrs_l)).astype(BF)
    send_all(RAG, lambda peer: rag_l.at[leaf], rag_l)
    loads[1].wait()
    sent_all(RRS, rrs_l)
    arrive_all(RAG, rag_l)

    rfp_l[panel] = nt(joined(rag_l)[:, :cols], root[...]).astype(BF)
    send_all(RFP, lambda peer: rfp_l.at[panel], rfp_l)
    sent_all(RAG, rag_l)
    arrive_all(RFP, rfp_l)
    root_forward = total(rfp_l)
    rf_out[...] = root_forward
    spread_blocks(srs_s, nn(root_forward.astype(BF), root[...]))
    send_all(SRS, lambda peer: srs_s.at[peer], srs_l)
    srs_l[leaf] = srs_s[leaf]
    sent_all(RFP, rfp_l)
    arrive_all(SRS, srs_l)
    sag_l[leaf] = total(srs_l).astype(BF)
    send_all(SAG, lambda peer: sag_l.at[leaf], sag_l)
    sent_all(SRS, srs_l)
    arrive_all(SAG, sag_l)
    root_half = joined(sag_l)[:, :cols]
    rs_out[...] = root_half.astype(F32)

    values = nn(root_half, oh_root[...]).astype(BF)
    for f in range(n_panel):
        ppan_s[f] = values[:, f * eblk:(f + 1) * eblk]
    send_all(PPAN, lambda peer: ppan_s.at[peer], ppan_l)
    ppan_l[panel] = ppan_s[panel]
    sent_all(SAG, sag_l)
    arrive_all(PPAN, ppan_l)
    pag_l[leaf] = total(ppan_l).astype(BF)
    send_all(PAG, lambda peer: pag_l.at[leaf], pag_l)
    sent_all(PPAN, ppan_l)
    arrive_all(PAG, pag_l)

    residual = forward[...] - nt(joined(pag_l), border[...])
    res_l[leaf] = residual.astype(BF)
    pair = leaf + 1 - 2 * lax.rem(leaf, 2)

    def hand_on(block):
        return pltpu.make_async_remote_copy(
            src_ref=res_l.at[block], dst_ref=res_l.at[block],
            send_sem=send_sem.at[RES, block + 1 - 2 * lax.rem(block, 2)],
            recv_sem=recv_sem.at[RES, block],
            device_id=(pair, panel), device_id_type=MESH,
        )

    def product(block):
        return nn(res_l[block], slab[pl.ds(pl.multiple_of(block * own, LANES), own), :])

    def direct_step(k, carry):
        copy(RES, res_l.at[leaf], res_l, lax.rem(leaf + 2 * k, n_leaf)).start()
        return carry

    lax.fori_loop(1, n_leaf // 2, direct_step, 0)
    hand_on(leaf).start()
    sent_all(PAG, pag_l)
    fs_out[...] = product(leaf)

    def relay_step(k, carry):
        source = lax.rem(leaf - 2 * k + n_leaf, n_leaf)
        arrived(RES, res_l, source)
        hand_on(source).start()
        fs_out[...] += product(source)
        return carry

    lax.fori_loop(1, n_leaf // 2, relay_step, 0)

    def pair_step(k, carry):
        source = lax.rem(pair - 2 * k + n_leaf, n_leaf)
        arrived(RES, res_l, source)
        fs_out[...] += product(source)
        return carry

    lax.fori_loop(0, n_leaf // 2, pair_step, 0)

    picks = nn(fs_out[...].astype(BF), oh_sub[...]).astype(BF)
    for s in range(n_leaf):
        picks_send[s] = picks[:, s * rows_sub:(s + 1) * rows_sub]
    send_all(PICK, lambda peer: picks_send.at[peer], pick_l)
    pick_l[leaf] = picks_send[leaf]
    sent_all(RES, res_l)
    arrive_all(PICK, pick_l)
    picked = jnp.where(living, total(pick_l), 0.0).astype(BF)
    su_out[...] = nn(picked, sc_ref[...])
    sent_all(PICK, pick_l)


def hand_out(rf_ref, rs_ref, fs_ref, su_ref, rf_out, rs_out, fs_out, su_out):
    rf_out[...] = rf_ref[...]
    rs_out[...] = rs_ref[...]
    fs_out[:, 0, :] = fs_ref[...]
    su_out[:, 0, :] = su_ref[...]


def fused(
    subtree_solution, subtree_coupling, sub_map, sub_count, front_rhs,
    sep_inverse, border_coupling, border_map, root_rhs, root_inverse,
):
    n_leaf, n_panel = lax.axis_size("leaf"), lax.axis_size("panel")
    batch = subtree_solution.shape[0]
    rows_sub, top = subtree_coupling.shape[1:]
    _, sep_width, own = sep_inverse.shape
    e_width = border_coupling.shape[2]
    eblk = e_width // n_leaf
    root_rows, cols = root_inverse.shape
    blk = ceil_to(-(-cols // n_leaf), LANES)
    vmem = pl.BlockSpec(memory_space=pltpu.VMEM)
    anywhere = pl.BlockSpec(memory_space=pl.ANY)
    smem = pl.BlockSpec(memory_space=pltpu.SMEM)

    def slots(n, width, dtype=BF, rows=batch):
        return pltpu.VMEM((n, rows, width), dtype)

    results = pl.pallas_call(
        functools.partial(kernel, n_leaf, n_panel),
        out_shape=(
            jax.ShapeDtypeStruct((batch, root_rows), F32),
            jax.ShapeDtypeStruct((batch, cols), F32),
            jax.ShapeDtypeStruct((batch, own), F32),
            jax.ShapeDtypeStruct((batch, top), F32),
        ),
        in_specs=[vmem, vmem, vmem, smem, vmem, vmem, vmem, anywhere, anywhere, anywhere],
        out_specs=(vmem,) * 4,
        scratch_shapes=[
            pltpu.VMEM((sep_width, own), BF),
            pltpu.VMEM((own, e_width), BF),
            pltpu.VMEM((root_rows, cols), BF),
            pltpu.VMEM((own, n_leaf * rows_sub), BF),
            pltpu.VMEM((cols, n_panel * eblk), BF),
            slots(n_leaf, blk, F32),
            pltpu.VMEM((batch, own), F32),
            slots(n_leaf, rows_sub),
            slots(n_leaf, rows_sub, BF, 2 * batch),
            slots(n_leaf, rows_sub, jnp.int32, 8),
            slots(n_leaf, own), slots(n_leaf, own),
            slots(n_leaf, eblk), slots(n_leaf, eblk),
            slots(n_panel, eblk),
            slots(n_leaf, blk), slots(n_leaf, blk), slots(n_leaf, blk),
            slots(n_panel, root_rows),
            slots(n_leaf, blk), slots(n_leaf, blk), slots(n_leaf, blk),
            slots(n_panel, eblk), slots(n_panel, eblk),
            slots(n_leaf, eblk),
            slots(n_leaf, own),
            slots(n_leaf, rows_sub),
            pltpu.SemaphoreType.DMA((n_leaf,)),
            pltpu.SemaphoreType.DMA((2,)),
            pltpu.SemaphoreType.DMA((14, max(n_leaf, n_panel))),
            pltpu.SemaphoreType.DMA((14, max(n_leaf, n_panel))),
        ],
        compiler_params=pltpu.CompilerParams(
            collective_id=0, has_side_effects=True, vmem_limit_bytes=VMEM_BYTES
        ),
    )(
        subtree_solution[:, 0, :], subtree_coupling[0], sub_map, sub_count, front_rhs,
        border_map, root_rhs, sep_inverse[0], border_coupling[0], root_inverse,
    )
    return pl.pallas_call(
        hand_out,
        out_shape=(
            jax.ShapeDtypeStruct((batch, root_rows), F32),
            jax.ShapeDtypeStruct((batch, cols), F32),
            jax.ShapeDtypeStruct((batch, 1, own), F32),
            jax.ShapeDtypeStruct((batch, 1, top), F32),
        ),
        in_specs=[vmem] * 4,
        out_specs=(vmem,) * 4,
    )(*results)


def fits(
    subtree_solution, subtree_coupling, sub_map, sub_count, front_rhs,
    sep_inverse, border_coupling, border_map, root_rhs, root_inverse,
):
    n_leaf = lax.axis_size("leaf")
    widths = (
        subtree_coupling.shape[1], subtree_coupling.shape[2], sep_inverse.shape[2],
        border_coupling.shape[2] // n_leaf, root_inverse.shape[0], root_inverse.shape[1],
    )
    small = (sep_inverse.size + border_coupling.size + root_inverse.size) * 2 < VMEM_BYTES * 6 // 10
    return (
        all(width % LANES == 0 for width in widths)
        and subtree_solution.shape[0] % 16 == 0
        and n_leaf % 2 == 0
        and small
    )


def program(*args):
    return fused(*args) if fits(*args) else body(*args)


def body(
    subtree_solution,
    subtree_coupling,
    sub_map,
    sub_count,
    front_rhs,
    sep_inverse,
    border_coupling,
    border_map,
    root_rhs,
    root_inverse,
):
    solved_values = subtree_solution[:, 0, :]
    coupling_factor = subtree_coupling[0]
    rows_sub = coupling_factor.shape[0]
    living = jnp.arange(rows_sub, dtype=jnp.int32) < sub_count[0, 0]
    contrib = lax.dot_general(
        solved_values, coupling_factor, (((1,), (1,)), ((), ())), preferred_element_type=jnp.float32
    )
    contrib = jnp.where(living[None, :], contrib, jnp.zeros_like(contrib))
    slab = sep_inverse[0]
    sep_width = slab.shape[0]
    batch = solved_values.shape[0]
    extended = jnp.zeros((batch, sep_width), jnp.float32).at[:, sub_map[0]].add(contrib)
    arrived = lax.psum_scatter(extended, "leaf", scatter_dimension=1, tiled=True)
    assembled = (front_rhs[:, 0, :] - arrived).astype(jnp.bfloat16)
    partial_rows = lax.dot_general(
        assembled, slab, (((1,), (1,)), ((), ())), preferred_element_type=jnp.float32
    )
    forward = lax.psum_scatter(partial_rows, "leaf", scatter_dimension=1, tiled=True)
    border_rows_local = border_coupling[0]
    partial_border = jnp.dot(
        forward.astype(jnp.bfloat16), border_rows_local, preferred_element_type=jnp.float32
    )
    border_term = lax.psum(partial_border, "leaf")
    panel_index = lax.axis_index("panel")
    col_width = root_rhs.shape[1]
    root_width = col_width * lax.axis_size("panel")
    own_map = border_map[panel_index]
    spread = jnp.zeros((batch, root_width), jnp.float32).at[:, own_map].add(border_term)
    root_term = lax.psum_scatter(spread, "panel", scatter_dimension=1, tiled=True)
    root_assembled = (root_rhs - root_term).astype(jnp.bfloat16)
    root_partial = lax.dot_general(
        root_assembled, root_inverse, (((1,), (1,)), ((), ())), preferred_element_type=jnp.float32
    )
    root_forward = lax.psum(root_partial, "panel")
    column_partial = jnp.dot(
        root_forward.astype(jnp.bfloat16), root_inverse, preferred_element_type=jnp.float32
    )
    root_solution = lax.psum(column_partial, "leaf")
    root_half = root_solution.astype(jnp.bfloat16)
    whole_root = lax.all_gather(root_half, "panel", axis=1, tiled=True)
    border_values = whole_root[:, own_map]
    correction = lax.dot_general(
        border_values,
        border_rows_local,
        (((1,), (1,)), ((), ())),
        preferred_element_type=jnp.float32,
    )
    residual = (forward - correction).astype(jnp.bfloat16)
    front_solution = jnp.dot(
        lax.all_gather(residual, "leaf", axis=1, tiled=True),
        slab,
        preferred_element_type=jnp.float32,
    )
    front_half = front_solution.astype(jnp.bfloat16)
    whole_front = lax.all_gather(front_half, "leaf", axis=1, tiled=True)
    picked = whole_front[:, sub_map[0]]
    picked = jnp.where(living[None, :], picked, jnp.zeros_like(picked))
    subtree_update = jnp.dot(picked, coupling_factor, preferred_element_type=jnp.float32)
    return (root_forward, root_solution, front_solution[:, None, :], subtree_update[:, None, :])


def solution(mesh):
    return jax.shard_map(
        program,
        mesh=mesh,
        in_specs=(
            P(None, "panel", "leaf"),
            P("panel", "leaf", None),
            P("panel", "leaf"),
            P("panel", "leaf"),
            P(None, "panel", "leaf"),
            P("panel", None, "leaf"),
            P("panel", "leaf", None),
            P(),
            P(None, "panel"),
            P("leaf", "panel"),
        ),
        out_specs=(
            P(None, "leaf"),
            P(None, "panel"),
            P(None, "panel", "leaf"),
            P(None, "panel", "leaf"),
        ),
        check_vma=False,
    )
```
